32 devices in a mesh: gx: 8 (over y, x, core), gy: 4 (over z).
Axes of the slice: x: 2, y: 2, z: 4, core: 2. Of those that a mesh axis runs over, the one named last changes fastest.
Arguments:
- charge_blocks: float32 [32768, 128], P(('gx', 'gy')), may hold values from -6 to 6
- block_tile: int32 [32768], P(('gx', 'gy')), may hold values from 0 to 49151, as said below
- block_count: int32 [32], P(('gx', 'gy')), may hold values from 512 to 1024, as said below
- near_kernel: float32 [9, 9, 9], replicated, may hold values from -0.21875 to 0.21875
- mid_kernel: float32 [9, 9, 9], replicated, may hold values from -0.109375 to 0.109375
- top_weights: float32 [4], replicated, may hold values from 0.0020412415 to 0.1
- top_widths: float32 [4], replicated, may hold values from 1 to 6
Outputs:
- potential: float32 [256, 96, 256], P('gx', 'gy')
The draws below stay inside these ranges and needn't reach their ends.
Inputs may be any that keep to these rules, and one draw needn't show every extreme that they name: `block_tile`: of the 1024 slots of one device, exactly 32 name tiles in the pencil of each device, dead slots included. Slots 0 to block_count - 1 of a device are live, the others hold values that are ignored.
All inputs are finite; a program needn't handle non-finite values.
Results may differ from the reference program's by a relative error of at most 0.000082.
Values sent between devices are 32-bit elements; how exact they have to be, the bound alone decides.
A program may use at most 128 MiB of HBM per device.

```python
import jax
import jax.numpy as jnp
from jax import lax

CX = 32
CY = 24
NZ = 256
CAP = 32
RADIUS = 4
ZB = 128
GAUSS = 4
NX = 256
NY = 96
BLK = 1024
SLOTS = 32768
N_GX = 8
N_GY = 4


def draw_block_tile(key, part):
    device_total = N_GX * N_GY
    subkeys = jax.random.split(jax.random.fold_in(key, 17), 5)
    owners = jnp.tile(jnp.arange(device_total, dtype=jnp.int32), CAP)
    destination = jax.vmap(lambda subkey: jax.random.permutation(subkey, owners))(jax.random.split(subkeys[0], device_total))
    local_x = jax.random.randint(subkeys[1], (device_total, BLK), 0, CX)
    local_y = jax.random.randint(subkeys[2], (device_total, BLK), 0, CY)
    local_z = jax.random.randint(subkeys[3], (device_total, BLK), 0, NZ // ZB)
    source = jnp.arange(device_total, dtype=jnp.int32)[:, None]
    special = jax.random.randint(subkeys[4], (), 0, device_total)
    top_hit = (source == special) & (destination == device_total - 1)
    low_hit = (source == special) & (destination == 0)
    local_x = jnp.where(top_hit, CX - 1, jnp.where(low_hit, 0, local_x))
    local_y = jnp.where(top_hit, CY - 1, jnp.where(low_hit, 0, local_y))
    local_z = jnp.where(top_hit, NZ // ZB - 1, jnp.where(low_hit, 0, local_z))
    global_x = destination // N_GY * CX + local_x
    global_y = destination % N_GY * CY + local_y
    tile_index = (global_x * NY + global_y) * (NZ // ZB) + local_z
    return tile_index.reshape(-1).astype(jnp.int32)


def draw_block_count(key, part):
    device_total = N_GX * N_GY
    subkeys = jax.random.split(jax.random.fold_in(key, 29), 3)
    counts = jax.random.randint(subkeys[0], (device_total,), BLK // 2, BLK + 1)
    fullest = jax.random.randint(subkeys[1], (), 0, device_total)
    emptiest = (fullest + 1 + jax.random.randint(subkeys[2], (), 0, device_total - 1)) % device_total
    device_ids = jnp.arange(device_total, dtype=jnp.int32)
    counts = jnp.where(device_ids == fullest, BLK, jnp.where(device_ids == emptiest, BLK // 2, counts))
    return counts.astype(jnp.int32)


def gaussian_terms(key):
    subkeys = jax.random.split(jax.random.fold_in(key, 41), 2)
    widest = jnp.float32(min(NX, NY, NZ) // 16)
    widths = jnp.exp(jax.random.uniform(subkeys[0], (GAUSS,), jnp.float32, 0.0, jnp.log(widest)))
    factors = jnp.exp(jax.random.uniform(subkeys[1], (GAUSS,), jnp.float32, jnp.log(0.03), jnp.log(0.1)))
    weights = factors / (widths * jnp.sqrt(widths))
    return (widths.astype(jnp.float32), weights.astype(jnp.float32))


def draw_top_widths(key, part):
    return gaussian_terms(key)[0]


def draw_top_weights(key, part):
    return gaussian_terms(key)[1]


def level_of(key, dims, cuts, low, largest):
    factor_of, own = 1.0, jax.random.fold_in(key, 6)
    for dim, shards_of in cuts:
        heights = jnp.exp(jax.random.uniform(jax.random.fold_in(own, dim), (shards_of,), jnp.float32, low / len(cuts), largest / len(cuts)))
        factor_of = factor_of * jnp.repeat(heights, dims[dim] // shards_of).reshape([-1 if axis == dim else 1 for axis in range(len(dims))])
    return factor_of


def gaussian(stream_key, shape, width, bound, shards=(), held_as=jnp.bfloat16):
    values = width * jax.random.normal(stream_key, shape, jnp.float32)
    if shards:
        values = values * level_of(stream_key, shape, shards, -0.22, 0.18)
    return jnp.clip(values, -bound, bound).astype(held_as)


def setup_inputs(seed: int = 0) -> dict:
    key_list = jax.random.split(jax.random.key(seed), 8)
    charge_blocks = gaussian(key_list[0], (SLOTS, ZB), 1.0, 6.0, ((0, 32),), jnp.float32)
    block_tile = draw_block_tile(jax.random.fold_in(key_list[7], 71), 0)
    block_count = draw_block_count(jax.random.fold_in(key_list[7], 71), 0)
    near_kernel = gaussian(key_list[3], (2 * RADIUS + 1, 2 * RADIUS + 1, 2 * RADIUS + 1), ((2 * RADIUS + 1) ** 3) ** -0.5, 0.21875, (), jnp.float32)
    mid_kernel = gaussian(key_list[4], (2 * RADIUS + 1, 2 * RADIUS + 1, 2 * RADIUS + 1), (4 * (2 * RADIUS + 1) ** 3) ** -0.5, 0.109375, (), jnp.float32)
    top_weights = draw_top_weights(jax.random.fold_in(key_list[7], 71), 0)
    top_widths = draw_top_widths(jax.random.fold_in(key_list[7], 71), 0)
    return dict(charge_blocks=charge_blocks, block_tile=block_tile, block_count=block_count, near_kernel=near_kernel, mid_kernel=mid_kernel, top_weights=top_weights, top_widths=top_widths)


PRECISE = lax.Precision.HIGHEST


def restrict_axis(values, axis_dim):
    before = jnp.roll(values, 1, axis_dim)
    behind = jnp.roll(values, -1, axis_dim)
    summed = values + 0.5 * (before + behind)
    return lax.slice_in_dim(summed, 0, values.shape[axis_dim], 2, axis_dim)


def restrict(values):
    return restrict_axis(restrict_axis(restrict_axis(values, 0), 1), 2)


def prolong_axis(coarse, axis_dim):
    following = jnp.roll(coarse, -1, axis_dim)
    paired = jnp.stack([coarse, 0.5 * (coarse + following)], axis=axis_dim + 1)
    layout = list(coarse.shape)
    layout[axis_dim] = 2 * layout[axis_dim]
    return paired.reshape(layout)


def prolong(coarse):
    return prolong_axis(prolong_axis(prolong_axis(coarse, 0), 1), 2)


def correlate(values, kernel):
    diameter = 2 * RADIUS + 1
    flipped = kernel[::-1, ::-1, ::-1]
    embedded = jnp.zeros(values.shape, jnp.float32).at[:diameter, :diameter, :diameter].set(flipped)
    embedded = jnp.roll(embedded, (-RADIUS, -RADIUS, -RADIUS), (0, 1, 2))
    spectrum = jnp.fft.rfftn(embedded) * jnp.fft.rfftn(values)
    return jnp.fft.irfftn(spectrum, s=values.shape).astype(jnp.float32)


def gaussians(period, widths, row_count):
    row_ids = jnp.arange(row_count, dtype=jnp.int32)[:, None]
    col_ids = jnp.arange(period, dtype=jnp.int32)[None, :]
    offset = (row_ids - col_ids) % period
    distance = jnp.minimum(offset, period - offset).astype(jnp.float32)
    return jnp.exp(-(distance * distance)[None] / (widths * widths)[:, None, None])


def top_level(top_charge, top_weights, top_widths):
    size_a, size_b, size_c = top_charge.shape
    gauss_x = gaussians(size_a, top_widths, size_a)
    gauss_y = gaussians(size_b, top_widths, size_b)
    gauss_z = gaussians(size_c, top_widths, size_c)
    along_x = jnp.einsum("kia,abc->kibc", gauss_x, top_charge, precision=PRECISE)
    along_y = jnp.einsum("kjb,kibc->kijc", gauss_y, along_x, precision=PRECISE)
    along_z = jnp.einsum("kzc,kijc->kijz", gauss_z, along_y, precision=PRECISE)
    return jnp.einsum("k,kijz->ijz", top_weights, along_z, precision=PRECISE)


def reference(charge_blocks, block_tile, block_count, near_kernel, mid_kernel, top_weights, top_widths):
    device_total = N_GX * N_GY
    slot_ids = jnp.arange(device_total * BLK, dtype=jnp.int32)
    owners = (slot_ids // BLK).astype(jnp.int32)
    live_slot = (slot_ids % BLK) < block_count[owners]
    masked = charge_blocks * live_slot[:, None].astype(jnp.float32)
    fine_charge = jax.ops.segment_sum(masked, block_tile, num_segments=NX * NY * (NZ // ZB)).reshape(NX, NY, NZ)
    mid_charge = restrict(fine_charge)
    top_charge = restrict(mid_charge)
    top_potential = top_level(top_charge, top_weights, top_widths)
    mid_potential = correlate(mid_charge, mid_kernel) + prolong(top_potential)
    return correlate(fine_charge, near_kernel) + prolong(mid_potential)
```

```python
import functools

import jax
import jax.numpy as jnp
from jax import lax
from jax.experimental import pallas as pl
from jax.experimental.pallas import tpu as pltpu
from jax.sharding import PartitionSpec as P

CX = 32
CY = 24
NZ = 256
RADIUS = 4
ZB = 128
DIAM = 2 * RADIUS + 1
IDROWS = 8


PRECISE = lax.Precision.HIGHEST
BF = jnp.bfloat16
F32 = jnp.float32
VMEM = pl.BlockSpec(memory_space=pltpu.VMEM)
SMEM = pl.BlockSpec(memory_space=pltpu.SMEM)


def params(mib):
    return pltpu.CompilerParams(vmem_limit_bytes=mib * 2**20)


def split2(values):
    high = values.astype(BF)
    low = (values - high.astype(F32)).astype(BF)
    return high, low


def split3(values):
    high = values.astype(BF)
    rest = values - high.astype(F32)
    mid = rest.astype(BF)
    return high, mid, (rest - mid.astype(F32)).astype(BF)


def mm(a, b):
    return jnp.dot(a, b, preferred_element_type=F32)


def iota(shape, dim):
    return lax.broadcasted_iota(jnp.int32, shape, dim)


def dispatch_kernel(devices, count_ref, owner_ref, tile_ref, charge_ref, out_ref, parts_ref):
    slots = charge_ref.shape[0]
    per_owner = slots // devices
    chunk = 512
    live = iota((slots, ZB), 0) < count_ref[0]
    high, mid, low = split3(jnp.where(live, charge_ref[...], 0.0))
    parts_ref[:, :ZB] = high
    parts_ref[:, ZB : 2 * ZB] = mid
    parts_ref[:, 2 * ZB :] = low
    upper = (iota((chunk, chunk), 0) < iota((chunk, chunk), 1)).astype(F32).astype(BF)
    before = jnp.zeros((devices, 1), F32)
    ranks = []
    tiles = jnp.zeros((devices, ZB), F32)
    for part in range(slots // chunk):
        lanes = slice(part * chunk, (part + 1) * chunk)
        owned = iota((devices, chunk), 0) == owner_ref[:, lanes]
        owned_f = owned.astype(F32)
        earlier = mm(owned_f.astype(BF), upper) + before
        before = before + jnp.sum(owned_f, axis=1, keepdims=True)
        rank = jnp.sum(jnp.where(owned, earlier, 0.0), axis=0, keepdims=True).astype(jnp.int32)
        ranks.append(rank)
        places = (iota((ZB, chunk), 0) == rank).astype(F32).astype(BF)
        ids = tile_ref[:, lanes]
        coarse = lax.shift_right_logical(ids, 6).astype(F32)
        fine = (ids & 63).astype(F32)
        across = (((1,), (1,)), ((), ()))
        for factor, value in ((64.0, coarse), (1.0, fine)):
            tiles = tiles + factor * lax.dot_general(
                (owned_f * value).astype(BF), places, across, preferred_element_type=F32
            )
    position = owner_ref[...] * per_owner + jnp.concatenate(ranks, axis=1)
    group = 256 // per_owner
    rows = group * per_owner

    def place(step, carry):
        chosen = (iota((rows, slots), 0) + step * rows == position).astype(F32).astype(BF)
        picked = mm(chosen, parts_ref[...])
        total = picked[:, :ZB] + (picked[:, ZB : 2 * ZB] + picked[:, 2 * ZB :])
        out_ref[pl.ds(step * group, group), :per_owner, :] = total.reshape(group, per_owner, ZB)
        return carry

    lax.fori_loop(0, devices // group, place, 0)
    out_ref[:, per_owner:, :] = jnp.broadcast_to(tiles[:, None, :], (devices, IDROWS, ZB))


def gather_kernel(ids_ref, arrived_ref, out_ref, parts_ref):
    devices, rows, _ = arrived_ref.shape
    per_owner = rows - IDROWS
    slots = devices * per_owner
    high, mid, low = split3(arrived_ref[:, :per_owner, :].reshape(slots, ZB))
    parts_ref[:, :ZB] = high
    parts_ref[:, ZB : 2 * ZB] = mid
    parts_ref[:, 2 * ZB :] = low
    tall = 8

    def add(step, carry):
        for stripe in range(NZ // ZB):
            first = stripe * CX * CY + step * tall * CX
            chosen = (iota((tall * CX, slots), 0) + first == ids_ref[...]).astype(F32).astype(BF)
            picked = mm(chosen, parts_ref[...])
            total = picked[:, :ZB] + (picked[:, ZB : 2 * ZB] + picked[:, 2 * ZB :])
            out_ref[pl.ds(step * tall, tall), :, stripe * ZB : (stripe + 1) * ZB] = total.reshape(
                tall, CX, ZB
            )
        return carry

    lax.fori_loop(0, CY // tall, add, 0)


def cutoff_kernel(tall, kernel_ref, padded_ref, out_ref, high_ref, low_ref, wide_ref, thin_ref):
    rows_y, rows_x, depth = out_ref.shape
    for a in range(DIAM):
        high, low = split2(padded_ref[:, a : a + rows_x, :])
        high_ref[:, :, a * depth : (a + 1) * depth] = high
        low_ref[:, :, a * depth : (a + 1) * depth] = low
    offset = iota((16, depth), 0) - iota((16, depth), 1) + RADIUS
    offset = jnp.where(offset < 0, offset + depth, offset)

    def shift(b, carry):
        for a in range(DIAM):
            base = jnp.zeros((16, depth), F32)
            for e in range(DIAM):
                base = jnp.where(offset == e, kernel_ref[(a * DIAM + b) * DIAM + e], base)
            base_high = base.astype(BF).astype(F32)
            base_low = base - base_high
            for i in range(depth // 16):
                at = slice(a * depth + 16 * i, a * depth + 16 * i + 16)
                wide_ref[at, :] = (pltpu.roll(base_high, 16 * i, 1) if i else base_high).astype(BF)
                thin_ref[at, :] = (pltpu.roll(base_low, 16 * i, 1) if i else base_low).astype(BF)

        def block(step, inner):
            at = pl.ds(step * tall + b, tall)
            high = high_ref[at].reshape(tall * rows_x, DIAM * depth)
            low = low_ref[at].reshape(tall * rows_x, DIAM * depth)
            part = mm(high, wide_ref[...]) + (mm(high, thin_ref[...]) + mm(low, wide_ref[...]))
            here = pl.ds(step * tall, tall)
            part = part.reshape(tall, rows_x, depth)

            @pl.when(b == 0)
            def _():
                out_ref[here] = part

            @pl.when(b > 0)
            def _():
                out_ref[here] += part

            return inner

        return lax.fori_loop(0, rows_y // tall, block, carry)

    lax.fori_loop(0, DIAM, shift, 0)


def cutoff(padded, kernel, tall):
    rows_y, rows_x, depth = padded.shape
    rows_y, rows_x = rows_y - 2 * RADIUS, rows_x - 2 * RADIUS
    wide = DIAM * depth
    return pl.pallas_call(
        functools.partial(cutoff_kernel, tall),
        out_shape=jax.ShapeDtypeStruct((rows_y, rows_x, depth), F32),
        in_specs=[SMEM, VMEM],
        out_specs=VMEM,
        scratch_shapes=[
            pltpu.VMEM((rows_y + 2 * RADIUS, rows_x, wide), BF),
            pltpu.VMEM((rows_y + 2 * RADIUS, rows_x, wide), BF),
            pltpu.VMEM((wide, depth), BF),
            pltpu.VMEM((wide, depth), BF),
        ],
        compiler_params=params(40),
        cost_estimate=pl.CostEstimate(
            flops=6 * rows_y * rows_x * depth * depth * DIAM * DIAM,
            bytes_accessed=8 * rows_y * rows_x * depth,
            transcendentals=0,
        ),
    )(kernel.reshape(-1), padded)


def extended_2(block, sides, width):
    for axis, dim in sides:
        count = lax.axis_size(axis)
        forward = [(i, i + 1) for i in range(count - 1)]
        forward.append((count - 1, 0))
        backward = [(target, source) for source, target in forward]
        low = lax.ppermute(
            lax.slice_in_dim(block, block.shape[dim] - width, None, axis=dim), axis, forward
        )
        high = lax.ppermute(lax.slice_in_dim(block, 0, width, axis=dim), axis, backward)
        block = jnp.concatenate([low, block, high], axis=dim)
    return block


def shifted(block, axis, distance):
    devices = range(lax.axis_size(axis))
    route = [((i - distance) % len(devices), i) for i in devices]
    return lax.ppermute(block, axis, route)


def widen(values):
    return extended_2(values, (("gx", 1), ("gy", 0)), RADIUS)


def wrap_depth(values):
    return jnp.concatenate([values[:, :, -1:], values, values[:, :, :1]], axis=2)


def thin_out(extended, axis_dim):
    length = extended.shape[axis_dim] - 2
    centre = lax.slice_in_dim(extended, 1, length + 1, 2, axis_dim)
    before = lax.slice_in_dim(extended, 0, length, 2, axis_dim)
    behind = lax.slice_in_dim(extended, 2, length + 2, 2, axis_dim)
    return centre + 0.5 * (before + behind)


def restrict(padded):
    row_count = padded.shape[0] - 2 * RADIUS
    col_count = padded.shape[1] - 2 * RADIUS
    inner = padded[RADIUS - 1 : RADIUS + row_count + 1, RADIUS - 1 : RADIUS + col_count + 1]
    halved = thin_out(inner, 0)
    halved = thin_out(halved, 1)
    return thin_out(wrap_depth(halved), 2)


def spread_next(extended, axis_dim):
    length = extended.shape[axis_dim] - 1
    centre = lax.slice_in_dim(extended, 0, length, 1, axis_dim)
    following = lax.slice_in_dim(extended, 1, length + 1, 1, axis_dim)
    paired = jnp.stack([centre, 0.5 * (centre + following)], axis=axis_dim + 1)
    layout = list(centre.shape)
    layout[axis_dim] = 2 * length
    return paired.reshape(layout)


def prolong(values):
    upper_row = shifted(values[:, :1], "gx", -1)
    taller = jnp.concatenate([values, upper_row], axis=1)
    upper_col = shifted(taller[:1], "gy", -1)
    padded = jnp.concatenate([taller, upper_col], axis=0)
    finer = spread_next(padded, 0)
    finer = spread_next(finer, 1)
    finer = jnp.concatenate([finer, finer[:, :, :1]], axis=2)
    return spread_next(finer, 2)


def gaussians(period, widths, first_row, row_count):
    row_ids = first_row + jnp.arange(row_count, dtype=jnp.int32)[:, None]
    col_ids = jnp.arange(period, dtype=jnp.int32)[None, :]
    offset = (row_ids - col_ids) % period
    distance = jnp.minimum(offset, period - offset).astype(jnp.float32)
    return jnp.exp(-(distance * distance)[None] / (widths * widths)[:, None, None])


def top_level(top_charge, top_weights, top_widths):
    rows_y, rows_x, depth_z = top_charge.shape
    period_x = rows_x * lax.axis_size("gx")
    period_y = rows_y * lax.axis_size("gy")
    gauss_x = gaussians(period_x, top_widths, lax.axis_index("gx") * rows_x, rows_x)
    gauss_y = gaussians(period_y, top_widths, lax.axis_index("gy") * rows_y, rows_y)
    gauss_z = gaussians(depth_z, top_widths, 0, depth_z)
    column = lax.all_gather(top_charge, "gx", axis=1, tiled=True)
    partial_rows = jnp.einsum("kia,bac->kbic", gauss_x, column, precision=PRECISE)
    plane = lax.all_gather(partial_rows, "gy", axis=1, tiled=True)
    along_y = jnp.einsum("kjb,kbic->kjic", gauss_y, plane, precision=PRECISE)
    along_z = jnp.einsum("kzc,kjic->kjiz", gauss_z, along_y, precision=PRECISE)
    return jnp.einsum("k,kjiz->jiz", top_weights, along_z, precision=PRECISE)


def fine_charges(charge_blocks, block_tile, block_count):
    size_x = lax.axis_size("gx")
    size_y = lax.axis_size("gy")
    device_total = size_x * size_y
    slot_total = charge_blocks.shape[0]
    per_owner = slot_total // device_total
    stripes = NZ // ZB
    grid_y = CY * size_y
    column_ids = block_tile // stripes
    stripe_ids = block_tile % stripes
    global_x = column_ids // grid_y
    global_y = column_ids % grid_y
    owner_ids = global_x // CX * size_y + global_y // CY
    local_tile = (stripe_ids * CY + global_y % CY) * CX + global_x % CX
    outgoing = pl.pallas_call(
        functools.partial(dispatch_kernel, device_total),
        out_shape=jax.ShapeDtypeStruct((device_total, per_owner + IDROWS, ZB), F32),
        in_specs=[SMEM, VMEM, VMEM, VMEM],
        out_specs=VMEM,
        scratch_shapes=[pltpu.VMEM((slot_total, 3 * ZB), BF)],
        compiler_params=params(40),
    )(block_count, owner_ids.reshape(1, -1), local_tile.reshape(1, -1), charge_blocks)
    arrived = lax.all_to_all(outgoing, ("gx", "gy"), split_axis=0, concat_axis=0, tiled=True)
    ids = arrived[:, per_owner, :per_owner].astype(jnp.int32).reshape(1, slot_total)
    return pl.pallas_call(
        gather_kernel,
        out_shape=jax.ShapeDtypeStruct((CY, CX, NZ), F32),
        in_specs=[VMEM, VMEM],
        out_specs=VMEM,
        scratch_shapes=[pltpu.VMEM((slot_total, 3 * ZB), BF)],
        compiler_params=params(40),
    )(ids, arrived)


def on_device(
    charge_blocks, block_tile, block_count, near_kernel, mid_kernel, top_weights, top_widths
):
    fine_charge = fine_charges(charge_blocks, block_tile, block_count)
    fine_padded = widen(fine_charge)
    mid_charge = restrict(fine_padded)
    mid_padded = widen(mid_charge)
    top_charge = restrict(mid_padded)
    top_potential = top_level(top_charge, top_weights, top_widths)
    mid_potential = cutoff(mid_padded, mid_kernel, 12) + prolong(top_potential)
    potential = cutoff(fine_padded, near_kernel, 8) + prolong(mid_potential)
    return jnp.transpose(potential, (1, 0, 2))


def solution(mesh):
    placed = (P(("gx", "gy"), None), P(("gx", "gy")), P(("gx", "gy")), P(), P(), P(), P())
    return jax.shard_map(
        on_device, mesh=mesh, in_specs=placed, out_specs=P("gx", "gy", None), check_vma=False
    )
```

```python
import functools

import jax
import jax.numpy as jnp
from jax import lax
from jax.experimental import pallas as pl
from jax.experimental.pallas import tpu as pltpu
from jax.sharding import PartitionSpec as P

CX = 32
CY = 24
NZ = 256
RADIUS = 4
ZB = 128
DIAM = 2 * RADIUS + 1
IDROWS = 8


PRECISE = lax.Precision.HIGHEST
BF = jnp.bfloat16
F32 = jnp.float32
VMEM = pl.BlockSpec(memory_space=pltpu.VMEM)
SMEM = pl.BlockSpec(memory_space=pltpu.SMEM)


def params(mib):
    return pltpu.CompilerParams(vmem_limit_bytes=mib * 2**20)


def split2(values):
    high = values.astype(BF)
    low = (values - high.astype(F32)).astype(BF)
    return high, low


def split3(values):
    high = values.astype(BF)
    rest = values - high.astype(F32)
    mid = rest.astype(BF)
    return high, mid, (rest - mid.astype(F32)).astype(BF)


def mm(a, b):
    return jnp.dot(a, b, preferred_element_type=F32)


def iota(shape, dim):
    return lax.broadcasted_iota(jnp.int32, shape, dim)


def dispatch_kernel(devices, count_ref, owner_ref, tile_ref, charge_ref, out_ref, parts_ref):
    slots = charge_ref.shape[0]
    per_owner = slots // devices
    chunk = 512
    live = iota((slots, ZB), 0) < count_ref[0]
    high, mid, low = split3(jnp.where(live, charge_ref[...], 0.0))
    parts_ref[:, :ZB] = high
    parts_ref[:, ZB : 2 * ZB] = mid
    parts_ref[:, 2 * ZB :] = low
    upper = (iota((chunk, chunk), 0) < iota((chunk, chunk), 1)).astype(F32).astype(BF)
    before = jnp.zeros((devices, 1), F32)
    ranks = []
    tiles = jnp.zeros((devices, ZB), F32)
    for part in range(slots // chunk):
        lanes = slice(part * chunk, (part + 1) * chunk)
        owned = iota((devices, chunk), 0) == owner_ref[:, lanes]
        owned_f = owned.astype(F32)
        earlier = mm(owned_f.astype(BF), upper) + before
        before = before + jnp.sum(owned_f, axis=1, keepdims=True)
        rank = jnp.sum(jnp.where(owned, earlier, 0.0), axis=0, keepdims=True).astype(jnp.int32)
        ranks.append(rank)
        places = (iota((ZB, chunk), 0) == rank).astype(F32).astype(BF)
        ids = tile_ref[:, lanes]
        coarse = lax.shift_right_logical(ids, 6).astype(F32)
        fine = (ids & 63).astype(F32)
        across = (((1,), (1,)), ((), ()))
        for factor, value in ((64.0, coarse), (1.0, fine)):
            tiles = tiles + factor * lax.dot_general(
                (owned_f * value).astype(BF), places, across, preferred_element_type=F32
            )
    position = owner_ref[...] * per_owner + jnp.concatenate(ranks, axis=1)
    group = 256 // per_owner
    rows = group * per_owner

    def place(step, carry):
        chosen = (iota((rows, slots), 0) + step * rows == position).astype(F32).astype(BF)
        picked = mm(chosen, parts_ref[...])
        total = picked[:, :ZB] + (picked[:, ZB : 2 * ZB] + picked[:, 2 * ZB :])
        out_ref[pl.ds(step * group, group), :per_owner, :] = total.reshape(group, per_owner, ZB)
        return carry

    lax.fori_loop(0, devices // group, place, 0)
    out_ref[:, per_owner:, :] = jnp.broadcast_to(tiles[:, None, :], (devices, IDROWS, ZB))


def gather_kernel(ids_ref, arrived_ref, out_ref, parts_ref):
    devices, rows, _ = arrived_ref.shape
    per_owner = rows - IDROWS
    slots = devices * per_owner
    high, mid, low = split3(arrived_ref[:, :per_owner, :].reshape(slots, ZB))
    parts_ref[:, :ZB] = high
    parts_ref[:, ZB : 2 * ZB] = mid
    parts_ref[:, 2 * ZB :] = low
    tall = 8

    def add(step, carry):
        for stripe in range(NZ // ZB):
            first = stripe * CX * CY + step * tall * CX
            chosen = (iota((tall * CX, slots), 0) + first == ids_ref[...]).astype(F32).astype(BF)
            picked = mm(chosen, parts_ref[...])
            total = picked[:, :ZB] + (picked[:, ZB : 2 * ZB] + picked[:, 2 * ZB :])
            out_ref[pl.ds(step * tall, tall), :, stripe * ZB : (stripe + 1) * ZB] = total.reshape(
                tall, CX, ZB
            )
        return carry

    lax.fori_loop(0, CY // tall, add, 0)


def cutoff_kernel(tall, kernel_ref, padded_ref, out_ref, high_ref, low_ref, wide_ref, thin_ref):
    rows_y, rows_x, depth = out_ref.shape
    for a in range(DIAM):
        high, low = split2(padded_ref[:, a : a + rows_x, :])
        high_ref[:, :, a * depth : (a + 1) * depth] = high
        low_ref[:, :, a * depth : (a + 1) * depth] = low
    offset = iota((16, depth), 0) - iota((16, depth), 1) + RADIUS
    offset = jnp.where(offset < 0, offset + depth, offset)

    def shift(b, carry):
        for a in range(DIAM):
            base = jnp.zeros((16, depth), F32)
            for e in range(DIAM):
                base = jnp.where(offset == e, kernel_ref[(a * DIAM + b) * DIAM + e], base)
            base_high = base.astype(BF).astype(F32)
            base_low = base - base_high
            for i in range(depth // 16):
                at = slice(a * depth + 16 * i, a * depth + 16 * i + 16)
                wide_ref[at, :] = (pltpu.roll(base_high, 16 * i, 1) if i else base_high).astype(BF)
                thin_ref[at, :] = (pltpu.roll(base_low, 16 * i, 1) if i else base_low).astype(BF)

        def block(step, inner):
            at = pl.ds(step * tall + b, tall)
            high = high_ref[at].reshape(tall * rows_x, DIAM * depth)
            low = low_ref[at].reshape(tall * rows_x, DIAM * depth)
            part = mm(high, wide_ref[...]) + (mm(high, thin_ref[...]) + mm(low, wide_ref[...]))
            here = pl.ds(step * tall, tall)
            part = part.reshape(tall, rows_x, depth)

            @pl.when(b == 0)
            def _():
                out_ref[here] = part

            @pl.when(b > 0)
            def _():
                out_ref[here] += part

            return inner

        return lax.fori_loop(0, rows_y // tall, block, carry)

    lax.fori_loop(0, DIAM, shift, 0)


def cutoff(padded, kernel, tall):
    rows_y, rows_x, depth = padded.shape
    rows_y, rows_x = rows_y - 2 * RADIUS, rows_x - 2 * RADIUS
    wide = DIAM * depth
    return pl.pallas_call(
        functools.partial(cutoff_kernel, tall),
        out_shape=jax.ShapeDtypeStruct((rows_y, rows_x, depth), F32),
        in_specs=[SMEM, VMEM],
        out_specs=VMEM,
        scratch_shapes=[
            pltpu.VMEM((rows_y + 2 * RADIUS, rows_x, wide), BF),
            pltpu.VMEM((rows_y + 2 * RADIUS, rows_x, wide), BF),
            pltpu.VMEM((wide, depth), BF),
            pltpu.VMEM((wide, depth), BF),
        ],
        compiler_params=params(40),
        cost_estimate=pl.CostEstimate(
            flops=6 * rows_y * rows_x * depth * depth * DIAM * DIAM,
            bytes_accessed=8 * rows_y * rows_x * depth,
            transcendentals=0,
        ),
    )(kernel.reshape(-1), padded)


def extended_2(block, low_width, high_width):
    for axis, dim in (("gx", 1), ("gy", 0)):
        count = lax.axis_size(axis)
        forward = [(i, (i + 1) % count) for i in range(count)]
        backward = [(target, source) for source, target in forward]
        low = lax.ppermute(
            lax.slice_in_dim(block, block.shape[dim] - low_width, None, axis=dim), axis, forward
        )
        high = lax.ppermute(lax.slice_in_dim(block, 0, high_width, axis=dim), axis, backward)
        block = jnp.concatenate([low, block, high], axis=dim)
    return block


def hat(distance):
    near = jnp.where(jnp.abs(distance) == 1, 0.5, 0.0)
    return jnp.where(distance == 0, 1.0, near)


def hat_periodic(shape, fine_dim):
    period = shape[fine_dim]
    distance = iota(shape, fine_dim) - 2 * iota(shape, 1 - fine_dim)
    distance = jnp.where(distance == 1 - period, 1, distance)
    distance = jnp.where(distance == period - 1, 1, distance)
    return hat(distance).astype(BF)


def exact_left(weights, values):
    high, mid, low = split3(values)
    return mm(weights, high) + (mm(weights, mid) + mm(weights, low))


def exact_right(values, weights):
    high, mid, low = split3(values)
    return mm(high, weights) + (mm(mid, weights) + mm(low, weights))


def restrict_kernel(padded_ref, out_ref):
    rows_y, rows_x, depth = out_ref.shape
    shape = (rows_x, padded_ref.shape[1])
    across = hat(iota(shape, 1) - RADIUS - 2 * iota(shape, 0)).astype(BF)
    lines = []
    for j in range(rows_y):
        centre = RADIUS + 2 * j
        line = padded_ref[centre] + 0.5 * (padded_ref[centre - 1] + padded_ref[centre + 1])
        lines.append(exact_left(across, line))
    along = hat_periodic((2 * depth, depth), 0)
    result = exact_right(jnp.concatenate(lines, axis=0), along)
    out_ref[...] = result.reshape(rows_y, rows_x, depth)


def restrict(padded, rows_y, rows_x):
    return pl.pallas_call(
        restrict_kernel,
        out_shape=jax.ShapeDtypeStruct((rows_y, rows_x, padded.shape[2] // 2), F32),
        in_specs=[VMEM],
        out_specs=VMEM,
        compiler_params=params(32),
    )(padded)


def hat_plane(rows, row_bits, cols, col_bits):
    row, col = iota((rows, cols), 0), iota((rows, cols), 1)
    step_y = lax.shift_right_logical(row, row_bits) - 2 * lax.shift_right_logical(col, col_bits)
    step_x = (row & (2**row_bits - 1)) - 2 * (col & (2**col_bits - 1))
    return (hat(step_y) * hat(step_x)).astype(BF)


def finish_kernel(plane_ref, along_ref, top_ref, mid_ref, fine_ref, out_ref):
    devices, top_y, top_x, depth = top_ref.shape
    top = top_ref[...].reshape(devices * top_y * top_x, depth)
    rows = plane_ref.shape[1]
    potential = jnp.zeros((rows, depth), F32)
    for k in range(plane_ref.shape[0]):
        term = jnp.dot(plane_ref[k], top, precision=PRECISE, preferred_element_type=F32)
        potential += jnp.dot(term, along_ref[k], precision=PRECISE, preferred_element_type=F32)
    mid_y, mid_x, mid_z = mid_ref.shape
    mid_rows = mid_y * mid_x
    coarse = exact_left(hat_plane(mid_rows, 5, rows, 4), potential)
    coarse = exact_right(coarse, hat_periodic((depth, mid_z), 1))
    middle = mid_ref[...].reshape(mid_rows, mid_z) + coarse
    fine_y, fine_x, fine_z = fine_ref.shape
    along = hat_periodic((mid_z, fine_z), 1)
    middle = exact_right(middle, along)
    finer = exact_left(hat_plane(fine_y * fine_x, 5, mid_rows, 5), middle)
    finer = finer.reshape(fine_y, fine_x, fine_z)
    for y in range(fine_y):
        out_ref[:, y, :] = fine_ref[y] + finer[y]


def wrapped(offset, period):
    offset = offset % period
    distance = jnp.minimum(offset, period - offset).astype(F32)
    return distance * distance


def top_tables(top_weights, top_widths):
    size_x, size_y = lax.axis_size("gx"), lax.axis_size("gy")
    top_x, top_y, depth = CX // 4, CY // 4, NZ // 4
    cols = jnp.arange(size_x * size_y * top_x * top_y, dtype=jnp.int32)
    owner = cols // (top_x * top_y)
    col_x = owner // size_y * top_x + cols % top_x
    col_y = owner % size_y * top_y + cols // top_x % top_y
    rows = jnp.arange((top_y + 1) * 16, dtype=jnp.int32)
    row_x = lax.axis_index("gx") * top_x + rows % 16
    row_y = lax.axis_index("gy") * top_y + rows // 16
    squares = wrapped(row_x[:, None] - col_x[None, :], size_x * top_x)
    squares = squares + wrapped(row_y[:, None] - col_y[None, :], size_y * top_y)
    widths = (top_widths * top_widths)[:, None, None]
    line = jnp.arange(depth, dtype=jnp.int32)
    along = jnp.exp(-wrapped(line[:, None] - line[None, :], depth)[None] / widths)
    return jnp.exp(-squares[None] / widths), top_weights[:, None, None] * along


def fine_charges(charge_blocks, block_tile, block_count):
    size_x = lax.axis_size("gx")
    size_y = lax.axis_size("gy")
    device_total = size_x * size_y
    slot_total = charge_blocks.shape[0]
    per_owner = slot_total // device_total
    stripes = NZ // ZB
    grid_y = CY * size_y
    column_ids = block_tile // stripes
    stripe_ids = block_tile % stripes
    global_x = column_ids // grid_y
    global_y = column_ids % grid_y
    owner_ids = global_x // CX * size_y + global_y // CY
    local_tile = (stripe_ids * CY + global_y % CY) * CX + global_x % CX
    outgoing = pl.pallas_call(
        functools.partial(dispatch_kernel, device_total),
        out_shape=jax.ShapeDtypeStruct((device_total, per_owner + IDROWS, ZB), F32),
        in_specs=[SMEM, VMEM, VMEM, VMEM],
        out_specs=VMEM,
        scratch_shapes=[pltpu.VMEM((slot_total, 3 * ZB), BF)],
        compiler_params=params(40),
    )(block_count, owner_ids.reshape(1, -1), local_tile.reshape(1, -1), charge_blocks)
    arrived = lax.all_to_all(outgoing, ("gx", "gy"), split_axis=0, concat_axis=0, tiled=True)
    ids = arrived[:, per_owner, :per_owner].astype(jnp.int32).reshape(1, slot_total)
    return pl.pallas_call(
        gather_kernel,
        out_shape=jax.ShapeDtypeStruct((CY, CX, NZ), F32),
        in_specs=[VMEM, VMEM],
        out_specs=VMEM,
        scratch_shapes=[pltpu.VMEM((slot_total, 3 * ZB), BF)],
        compiler_params=params(40),
    )(ids, arrived)


def on_device(
    charge_blocks, block_tile, block_count, near_kernel, mid_kernel, top_weights, top_widths
):
    fine_charge = fine_charges(charge_blocks, block_tile, block_count)
    plane, along = top_tables(top_weights, top_widths)
    fine_padded = extended_2(fine_charge, RADIUS, RADIUS)
    mid_charge = restrict(fine_padded, CY // 2, CX // 2)
    mid_padded = extended_2(mid_charge, RADIUS, RADIUS + 1)
    spare = CX + 2 * RADIUS - mid_padded.shape[1]
    mid_padded = jnp.pad(mid_padded, ((0, 0), (0, spare), (0, 0)))
    top_charge = restrict(mid_padded, CY // 4, CX // 4)
    top_all = lax.all_gather(top_charge, ("gx", "gy"), axis=0, tiled=False)
    mid_cut = cutoff(mid_padded, mid_kernel, CY // 2 + 1)
    fine_cut = cutoff(fine_padded, near_kernel, 8)
    return pl.pallas_call(
        finish_kernel,
        out_shape=jax.ShapeDtypeStruct((CX, CY, NZ), F32),
        in_specs=[VMEM] * 5,
        out_specs=VMEM,
        compiler_params=params(48),
    )(plane, along, top_all, mid_cut, fine_cut)


def solution(mesh):
    placed = (P(("gx", "gy"), None), P(("gx", "gy")), P(("gx", "gy")), P(), P(), P(), P())
    return jax.shard_map(
        on_device, mesh=mesh, in_specs=placed, out_specs=P("gx", "gy", None), check_vma=False
    )
```

```python
import functools

import jax
import jax.numpy as jnp
from jax import lax
from jax.experimental import pallas as pl
from jax.experimental.pallas import tpu as pltpu
from jax.sharding import PartitionSpec as P

CX = 32
CY = 24
NZ = 256
RADIUS = 4
ZB = 128
DIAM = 2 * RADIUS + 1
IDROWS = 8


PRECISE = lax.Precision.HIGHEST
BF = jnp.bfloat16
F32 = jnp.float32
VMEM = pl.BlockSpec(memory_space=pltpu.VMEM)
SMEM = pl.BlockSpec(memory_space=pltpu.SMEM)


def params(mib):
    return pltpu.CompilerParams(vmem_limit_bytes=mib * 2**20)


def split2(values):
    high = values.astype(BF)
    low = (values - high.astype(F32)).astype(BF)
    return high, low


def split3(values):
    high = values.astype(BF)
    rest = values - high.astype(F32)
    mid = rest.astype(BF)
    return high, mid, (rest - mid.astype(F32)).astype(BF)


def mm(a, b):
    return jnp.dot(a, b, preferred_element_type=F32)


def iota(shape, dim):
    return lax.broadcasted_iota(jnp.int32, shape, dim)


def dispatch_kernel(devices, count_ref, owner_ref, tile_ref, charge_ref, out_ref, parts_ref):
    slots = charge_ref.shape[0]
    per_owner = slots // devices
    chunk = 512
    live = iota((slots, ZB), 0) < count_ref[0]
    high, mid, low = split3(jnp.where(live, charge_ref[...], 0.0))
    parts_ref[:, :ZB] = high
    parts_ref[:, ZB : 2 * ZB] = mid
    parts_ref[:, 2 * ZB :] = low
    upper = (iota((chunk, chunk), 0) < iota((chunk, chunk), 1)).astype(F32).astype(BF)
    before = jnp.zeros((devices, 1), F32)
    ranks = []
    tiles = jnp.zeros((devices, ZB), F32)
    for part in range(slots // chunk):
        lanes = slice(part * chunk, (part + 1) * chunk)
        owned = iota((devices, chunk), 0) == owner_ref[:, lanes]
        owned_f = owned.astype(F32)
        earlier = mm(owned_f.astype(BF), upper) + before
        before = before + jnp.sum(owned_f, axis=1, keepdims=True)
        rank = jnp.sum(jnp.where(owned, earlier, 0.0), axis=0, keepdims=True).astype(jnp.int32)
        ranks.append(rank)
        places = (iota((ZB, chunk), 0) == rank).astype(F32).astype(BF)
        ids = tile_ref[:, lanes]
        coarse = lax.shift_right_logical(ids, 6).astype(F32)
        fine = (ids & 63).astype(F32)
        across = (((1,), (1,)), ((), ()))
        for factor, value in ((64.0, coarse), (1.0, fine)):
            tiles = tiles + factor * lax.dot_general(
                (owned_f * value).astype(BF), places, across, preferred_element_type=F32
            )
    position = owner_ref[...] * per_owner + jnp.concatenate(ranks, axis=1)
    group = 256 // per_owner
    rows = group * per_owner

    def place(step, carry):
        chosen = (iota((rows, slots), 0) + step * rows == position).astype(F32).astype(BF)
        picked = mm(chosen, parts_ref[...])
        total = picked[:, :ZB] + (picked[:, ZB : 2 * ZB] + picked[:, 2 * ZB :])
        out_ref[pl.ds(step * group, group), :per_owner, :] = total.reshape(group, per_owner, ZB)
        return carry

    lax.fori_loop(0, devices // group, place, 0)
    out_ref[:, per_owner:, :] = jnp.broadcast_to(tiles[:, None, :], (devices, IDROWS, ZB))


def gather_kernel(ids_ref, arrived_ref, out_ref, parts_ref):
    devices, rows, _ = arrived_ref.shape
    per_owner = rows - IDROWS
    slots = devices * per_owner
    high, mid, low = split3(arrived_ref[:, :per_owner, :].reshape(slots, ZB))
    parts_ref[:, :ZB] = high
    parts_ref[:, ZB : 2 * ZB] = mid
    parts_ref[:, 2 * ZB :] = low
    tall = 8

    def add(step, carry):
        for stripe in range(NZ // ZB):
            first = stripe * CX * CY + step * tall * CX
            chosen = (iota((tall * CX, slots), 0) + first == ids_ref[...]).astype(F32).astype(BF)
            picked = mm(chosen, parts_ref[...])
            total = picked[:, :ZB] + (picked[:, ZB : 2 * ZB] + picked[:, 2 * ZB :])
            out_ref[pl.ds(step * tall, tall), :, stripe * ZB : (stripe + 1) * ZB] = total.reshape(
                tall, CX, ZB
            )
        return carry

    lax.fori_loop(0, CY // tall, add, 0)


def cutoff_kernel(tall, kernel_ref, padded_ref, out_ref, high_ref, low_ref, wide_ref, thin_ref):
    rows_y, rows_x, depth = out_ref.shape
    for a in range(DIAM):
        high, low = split2(padded_ref[:, a : a + rows_x, :])
        high_ref[:, :, a * depth : (a + 1) * depth] = high
        low_ref[:, :, a * depth : (a + 1) * depth] = low
    offset = iota((16, depth), 0) - iota((16, depth), 1) + RADIUS
    offset = jnp.where(offset < 0, offset + depth, offset)

    def shift(b, carry):
        for a in range(DIAM):
            base = jnp.zeros((16, depth), F32)
            for e in range(DIAM):
                base = jnp.where(offset == e, kernel_ref[(a * DIAM + b) * DIAM + e], base)
            base_high = base.astype(BF).astype(F32)
            base_low = base - base_high
            for i in range(depth // 16):
                at = slice(a * depth + 16 * i, a * depth + 16 * i + 16)
                wide_ref[at, :] = (pltpu.roll(base_high, 16 * i, 1) if i else base_high).astype(BF)
                thin_ref[at, :] = (pltpu.roll(base_low, 16 * i, 1) if i else base_low).astype(BF)

        def block(step, inner):
            at = pl.ds(step * tall + b, tall)
            high = high_ref[at].reshape(tall * rows_x, DIAM * depth)
            low = low_ref[at].reshape(tall * rows_x, DIAM * depth)
            part = mm(high, wide_ref[...]) + (mm(high, thin_ref[...]) + mm(low, wide_ref[...]))
            here = pl.ds(step * tall, tall)
            part = part.reshape(tall, rows_x, depth)

            @pl.when(b == 0)
            def _():
                out_ref[here] = part

            @pl.when(b > 0)
            def _():
                out_ref[here] += part

            return inner

        return lax.fori_loop(0, rows_y // tall, block, carry)

    lax.fori_loop(0, DIAM, shift, 0)


def cutoff(padded, kernel, tall):
    rows_y, rows_x, depth = padded.shape
    rows_y, rows_x = rows_y - 2 * RADIUS, rows_x - 2 * RADIUS
    wide = DIAM * depth
    return pl.pallas_call(
        functools.partial(cutoff_kernel, tall),
        out_shape=jax.ShapeDtypeStruct((rows_y, rows_x, depth), F32),
        in_specs=[SMEM, VMEM],
        out_specs=VMEM,
        scratch_shapes=[
            pltpu.VMEM((rows_y + 2 * RADIUS, rows_x, wide), BF),
            pltpu.VMEM((rows_y + 2 * RADIUS, rows_x, wide), BF),
            pltpu.VMEM((wide, depth), BF),
            pltpu.VMEM((wide, depth), BF),
        ],
        compiler_params=params(40),
        cost_estimate=pl.CostEstimate(
            flops=6 * rows_y * rows_x * depth * depth * DIAM * DIAM,
            bytes_accessed=8 * rows_y * rows_x * depth,
            transcendentals=0,
        ),
    )(kernel.reshape(-1), padded)


def extended_2(block, low_width, high_width):
    for axis, dim in (("gx", 1), ("gy", 0)):
        count = lax.axis_size(axis)
        forward = [(i, (i + 1) % count) for i in range(count)]
        backward = [(target, source) for source, target in forward]
        low = lax.ppermute(
            lax.slice_in_dim(block, block.shape[dim] - low_width, None, axis=dim), axis, forward
        )
        high = lax.ppermute(lax.slice_in_dim(block, 0, high_width, axis=dim), axis, backward)
        block = jnp.concatenate([low, block, high], axis=dim)
    return block


def hat(distance):
    near = jnp.where(jnp.abs(distance) == 1, 0.5, 0.0)
    return jnp.where(distance == 0, 1.0, near)


def hat_periodic(shape, fine_dim):
    period = shape[fine_dim]
    distance = iota(shape, fine_dim) - 2 * iota(shape, 1 - fine_dim)
    distance = jnp.where(distance == 1 - period, 1, distance)
    distance = jnp.where(distance == period - 1, 1, distance)
    return hat(distance).astype(BF)


def exact_left(weights, values):
    high, mid, low = split3(values)
    return mm(weights, high) + (mm(weights, mid) + mm(weights, low))


def exact_right(values, weights):
    high, mid, low = split3(values)
    return mm(high, weights) + (mm(mid, weights) + mm(low, weights))


def restrict_kernel(padded_ref, out_ref):
    rows_y, rows_x, depth = out_ref.shape
    shape = (rows_x, padded_ref.shape[1])
    across = hat(iota(shape, 1) - RADIUS - 2 * iota(shape, 0)).astype(BF)
    lines = []
    for j in range(rows_y):
        centre = RADIUS + 2 * j
        line = padded_ref[centre] + 0.5 * (padded_ref[centre - 1] + padded_ref[centre + 1])
        lines.append(exact_left(across, line))
    along = hat_periodic((2 * depth, depth), 0)
    result = exact_right(jnp.concatenate(lines, axis=0), along)
    out_ref[...] = result.reshape(rows_y, rows_x, depth)


def restrict(padded, rows_y, rows_x):
    return pl.pallas_call(
        restrict_kernel,
        out_shape=jax.ShapeDtypeStruct((rows_y, rows_x, padded.shape[2] // 2), F32),
        in_specs=[VMEM],
        out_specs=VMEM,
        compiler_params=params(32),
    )(padded)


def hat_plane(rows, row_bits, cols, col_bits):
    row, col = iota((rows, cols), 0), iota((rows, cols), 1)
    step_y = lax.shift_right_logical(row, row_bits) - 2 * lax.shift_right_logical(col, col_bits)
    step_x = (row & (2**row_bits - 1)) - 2 * (col & (2**col_bits - 1))
    return (hat(step_y) * hat(step_x)).astype(BF)


def finish_kernel(plane_ref, along_ref, top_ref, mid_ref, fine_ref, out_ref):
    devices, top_y, top_x, depth = top_ref.shape
    top = top_ref[...].reshape(devices * top_y * top_x, depth)
    rows = plane_ref.shape[1]
    potential = jnp.zeros((rows, depth), F32)
    for k in range(plane_ref.shape[0]):
        term = jnp.dot(plane_ref[k], top, precision=PRECISE, preferred_element_type=F32)
        potential += jnp.dot(term, along_ref[k], precision=PRECISE, preferred_element_type=F32)
    mid_y, mid_x, mid_z = mid_ref.shape
    mid_rows = mid_y * mid_x
    coarse = exact_left(hat_plane(mid_rows, 5, rows, 4), potential)
    coarse = exact_right(coarse, hat_periodic((depth, mid_z), 1))
    middle = mid_ref[...].reshape(mid_rows, mid_z) + coarse
    fine_y, fine_x, fine_z = fine_ref.shape
    along = hat_periodic((mid_z, fine_z), 1)
    middle = exact_right(middle, along)
    finer = exact_left(hat_plane(fine_y * fine_x, 5, mid_rows, 5), middle)
    finer = finer.reshape(fine_y, fine_x, fine_z)
    for y in range(fine_y):
        out_ref[:, y, :] = fine_ref[y] + finer[y]


def wrapped(offset, period):
    offset = offset % period
    distance = jnp.minimum(offset, period - offset).astype(F32)
    return distance * distance


def top_tables(top_weights, top_widths):
    size_x, size_y = lax.axis_size("gx"), lax.axis_size("gy")
    top_x, top_y, depth = CX // 4, CY // 4, NZ // 4
    cols = jnp.arange(size_x * size_y * top_x * top_y, dtype=jnp.int32)
    owner = cols // (top_x * top_y)
    col_x = owner % size_x * top_x + cols % top_x
    col_y = owner // size_x * top_y + cols // top_x % top_y
    rows = jnp.arange((top_y + 1) * 16, dtype=jnp.int32)
    row_x = lax.axis_index("gx") * top_x + rows % 16
    row_y = lax.axis_index("gy") * top_y + rows // 16
    squares = wrapped(row_x[:, None] - col_x[None, :], size_x * top_x)
    squares = squares + wrapped(row_y[:, None] - col_y[None, :], size_y * top_y)
    widths = (top_widths * top_widths)[:, None, None]
    line = jnp.arange(depth, dtype=jnp.int32)
    along = jnp.exp(-wrapped(line[:, None] - line[None, :], depth)[None] / widths)
    return jnp.exp(-squares[None] / widths), top_weights[:, None, None] * along


def fine_charges(charge_blocks, block_tile, block_count):
    size_x = lax.axis_size("gx")
    size_y = lax.axis_size("gy")
    device_total = size_x * size_y
    slot_total = charge_blocks.shape[0]
    per_owner = slot_total // device_total
    stripes = NZ // ZB
    grid_y = CY * size_y
    column_ids = block_tile // stripes
    stripe_ids = block_tile % stripes
    global_x = column_ids // grid_y
    global_y = column_ids % grid_y
    owner_ids = global_x // CX * size_y + global_y // CY
    local_tile = (stripe_ids * CY + global_y % CY) * CX + global_x % CX
    outgoing = pl.pallas_call(
        functools.partial(dispatch_kernel, device_total),
        out_shape=jax.ShapeDtypeStruct((device_total, per_owner + IDROWS, ZB), F32),
        in_specs=[SMEM, VMEM, VMEM, VMEM],
        out_specs=VMEM,
        scratch_shapes=[pltpu.VMEM((slot_total, 3 * ZB), BF)],
        compiler_params=params(40),
    )(block_count, owner_ids.reshape(1, -1), local_tile.reshape(1, -1), charge_blocks)
    arrived = lax.all_to_all(outgoing, ("gx", "gy"), split_axis=0, concat_axis=0, tiled=True)
    ids = arrived[:, per_owner, :per_owner].astype(jnp.int32).reshape(1, slot_total)
    return pl.pallas_call(
        gather_kernel,
        out_shape=jax.ShapeDtypeStruct((CY, CX, NZ), F32),
        in_specs=[VMEM, VMEM],
        out_specs=VMEM,
        scratch_shapes=[pltpu.VMEM((slot_total, 3 * ZB), BF)],
        compiler_params=params(40),
    )(ids, arrived)


def on_device(
    charge_blocks, block_tile, block_count, near_kernel, mid_kernel, top_weights, top_widths
):
    fine_charge = fine_charges(charge_blocks, block_tile, block_count)
    plane, along = top_tables(top_weights, top_widths)
    fine_padded = extended_2(fine_charge, RADIUS, RADIUS)
    mid_charge = restrict(fine_padded, CY // 2, CX // 2)
    mid_padded = extended_2(mid_charge, RADIUS, RADIUS + 1)
    spare = CX + 2 * RADIUS - mid_padded.shape[1]
    mid_padded = jnp.pad(mid_padded, ((0, 0), (0, spare), (0, 0)))
    top_charge = restrict(mid_padded, CY // 4, CX // 4)
    top_all = lax.all_gather(top_charge[None], "gx", axis=0, tiled=True)
    top_all = lax.all_gather(top_all, "gy", axis=0, tiled=True)
    mid_cut = cutoff(mid_padded, mid_kernel, CY // 2 + 1)
    fine_cut = cutoff(fine_padded, near_kernel, 8)
    return pl.pallas_call(
        finish_kernel,
        out_shape=jax.ShapeDtypeStruct((CX, CY, NZ), F32),
        in_specs=[VMEM] * 5,
        out_specs=VMEM,
        compiler_params=params(48),
    )(plane, along, top_all, mid_cut, fine_cut)


def solution(mesh):
    placed = (P(("gx", "gy"), None), P(("gx", "gy")), P(("gx", "gy")), P(), P(), P(), P())
    return jax.shard_map(
        on_device, mesh=mesh, in_specs=placed, out_specs=P("gx", "gy", None), check_vma=False
    )
```
